32 devices in a mesh: grp: 2 (over x), blk: 16 (over z, y, core).
Axes of the slice: x: 2, y: 2, z: 4, core: 2. Of those that a mesh axis runs over, the one named last changes fastest.
Arguments:
- parent_rows: bfloat16 [32, 12288], P(('grp', 'blk')), parts along dimension 0, may hold values from -3 to 3
- token_rows: bfloat16 [64, 12288], P(('grp', 'blk')), parts along dimension 0, may hold values from -3 to 3
- parent: int32 [64], P('grp'), parts along dimension 0, may hold values from 0 to 15
- d_hidden: bfloat16 [64, 2048], P('grp', 'blk'), parts along dimension 0, may hold values from -3 to 3
- w_gate: bfloat16 [12288, 2048], P(None, 'blk'), may hold values from -0.0546875 to 0.0546875
- w_up: bfloat16 [12288, 2048], P(None, 'blk'), may hold values from -0.0546875 to 0.0546875
Outputs:
- grad_gate: bfloat16 [12288, 4096], P(None, ('grp', 'blk')), parts along dimension 1
- grad_up: bfloat16 [12288, 4096], P(None, ('grp', 'blk')), parts along dimension 1
- grad_parent: bfloat16 [32, 12288], P(('grp', 'blk')), parts along dimension 0
The draws below stay inside these ranges and needn't reach their ends.
There are 2 independent parts, one for each index of `grp`. The reference program is written for one: setup_inputs(seed, part) draws one part's arguments, and reference() takes and returns one part's arrays. A program takes and returns all parts, laid end to end along the dimension named above; an argument that names none is the same for every part. Nothing has to cross between parts.
Inputs may be any that keep to these rules, and one draw needn't show every extreme that they name: Each hypothesis row names its parent among the 16 parent rows.
All inputs are finite; a program needn't handle non-finite values.
Results may differ from the reference program's by a relative error of at most 0.0069.
Values may be sent and summed in bfloat16 or wider, within the bound.
No kernel may reach another device: no remote copies, remote signals or barrier semaphores. Data moves between devices by JAX's collectives and lax.ppermute only.
A program may use at most 128 MiB of HBM per device.

```python
import math
import jax
import jax.numpy as jnp
import numpy as np

D = 12288
HIDDEN_SIZE = 2048
PARENTS = 16
HYP = 32


def plant(result, key, least, high):
    spot = [jax.random.randint(jax.random.fold_in(key, axis), (), 0, length) for axis, length in enumerate(result.shape)]
    longest = result.shape.index(max(result.shape))
    neighbour = spot[:longest] + [(spot[longest] + 1) % result.shape[longest]] + spot[longest + 1:]
    return result.at[tuple(spot)].set(least).at[tuple(neighbour)].set(high)


def steps_of(rng, extent, shards, low, high):
    factor_of = 1.0
    for axis_at, shards_of in shards:
        steps = jax.random.uniform(jax.random.fold_in(jax.random.fold_in(rng, 6), axis_at), (shards_of,), jnp.float32, low / len(shards), high / len(shards))
        factor_of = factor_of * jnp.repeat(jnp.exp(steps), extent[axis_at] // shards_of).reshape((-1,) + (1,) * (len(extent) - 1 - axis_at))
    return factor_of


def cumulative_ranks(number_of, lean):
    portions = [(1 << 20) // math.isqrt(standing ** lean) + 1 for standing in range(1, number_of + 1)]
    spread = 1 + sum(portions) // (1 << 30)
    return np.cumsum(np.array([max(1, weight // spread) for weight in portions]))


def ranked(rng, dims, amount, lean):
    listing = cumulative_ranks(amount, lean)
    lot = jax.random.randint(jax.random.fold_in(rng, 1), dims, 0, int(listing[amount - 1]))
    rank = jnp.searchsorted(jnp.asarray(listing, jnp.int32), lot, side="right")
    return jax.random.permutation(jax.random.fold_in(rng, 2), amount)[rank].astype(jnp.int32)


def gaussian(key, extent, width, limit, pieces=(), held_as=jnp.bfloat16):
    values = width * jax.random.normal(key, extent, jnp.float32)
    if pieces:
        values = values * steps_of(key, extent, pieces, -0.22, 0.18)
    return jnp.clip(values, -limit, limit).astype(held_as)


def setup_inputs(seed: int = 0, part: int = 0) -> dict:
    streams_of = jax.random.split(jax.random.key(seed), 7)
    part_keys = jax.random.split(jax.random.fold_in(streams_of[6], part), 7)
    return {
        "parent_rows": gaussian(part_keys[0], (PARENTS, D), 0.5, 3.0, ((0, 16),)),
        "token_rows": gaussian(part_keys[1], (HYP, D), 0.5, 3.0, ((0, 16),)),
        "parent": plant(ranked(part_keys[2], (HYP,), PARENTS, 2), jax.random.fold_in(part_keys[2], 3), 0, PARENTS - 1).astype(jnp.int32),
        "d_hidden": gaussian(part_keys[3], (HYP, HIDDEN_SIZE), 0.3, 3.0, ((1, 16),)),
        "w_gate": gaussian(streams_of[4], (D, HIDDEN_SIZE), D ** -0.5, 0.0546875, ((1, 16),)),
        "w_up": gaussian(streams_of[5], (D, HIDDEN_SIZE), D ** -0.5, 0.0546875, ((1, 16),)),
    }


def reference(parent_rows, token_rows, parent, d_hidden, w_gate, w_up):
    picked = jnp.take(parent_rows, parent, axis=0).astype(jnp.float32)
    inputs = (picked + token_rows.astype(jnp.float32)).astype(jnp.bfloat16)
    gate = jnp.dot(inputs, w_gate, preferred_element_type=jnp.float32)
    up = jnp.dot(inputs, w_up, preferred_element_type=jnp.float32)
    sig = jax.nn.sigmoid(gate)
    upstream = d_hidden.astype(jnp.float32)
    d_gate = (upstream * up * sig * (1.0 + gate * (1.0 - sig))).astype(jnp.bfloat16)
    d_up = (upstream * gate * sig).astype(jnp.bfloat16)
    grad_gate = jnp.dot(inputs.T, d_gate, preferred_element_type=jnp.float32).astype(jnp.bfloat16)
    grad_up = jnp.dot(inputs.T, d_up, preferred_element_type=jnp.float32).astype(jnp.bfloat16)
    parent_gate = jax.ops.segment_sum(d_gate.astype(jnp.float32), parent, PARENTS).astype(jnp.bfloat16)
    parent_up = jax.ops.segment_sum(d_up.astype(jnp.float32), parent, PARENTS).astype(jnp.bfloat16)
    total = jnp.dot(parent_gate, w_gate.T, preferred_element_type=jnp.float32)
    total = total + jnp.dot(parent_up, w_up.T, preferred_element_type=jnp.float32)
    return grad_gate, grad_up, total.astype(jnp.bfloat16)
```

```python
import jax
import jax.numpy as jnp
from jax import lax
from jax.sharding import PartitionSpec as P

BF = jnp.bfloat16
F32 = jnp.float32


def factors(count):
    chips = count // 2
    bits = chips.bit_length() - 1
    outer = 1 << ((bits + 1) // 2)
    return outer, chips // outer, 2


def partner(mask, count):
    return [(i, i ^ mask) for i in range(count)]


def slot_masks(count):
    outer, inner, _ = factors(count)
    return [(z * inner + y) * 2 + c for c in range(2) for y in range(inner) for z in range(outer)]


def gather(block, count):
    outer, inner, _ = factors(count)
    send = lambda x, mask: lax.ppermute(x, "blk", partner(mask, count))
    column = jnp.concatenate([block] + [send(block, z * inner * 2) for z in range(1, outer)], 0)
    plane = jnp.concatenate([column] + [send(column, y * 2) for y in range(1, inner)], 0)
    return jnp.concatenate([plane, send(plane, 1)], 0)


def scatter(terms, count):
    outer, inner, _ = factors(count)
    send = lambda x, mask: lax.ppermute(x, "blk", partner(mask, count))
    half = count
    low, high = terms[:half], terms[half:].astype(BF)
    total = low + send(high, 1).astype(F32)
    step = outer * 2
    rows = total[:step]
    for y in range(1, inner):
        rows = rows + send(total[y * step:(y + 1) * step].astype(BF), y * 2).astype(F32)
    own = rows[:2]
    for z in range(1, outer):
        own = own + send(rows[2 * z:2 * z + 2].astype(BF), z * inner * 2).astype(F32)
    return own


def body(parent_rows, token_rows, parent, d_hidden, w_gate, w_up):
    count = lax.axis_size("blk")
    width = token_rows.shape[1]
    half = width // 2
    hyp = parent.shape[0]
    me = lax.axis_index("blk")
    block = jnp.concatenate([token_rows, parent_rows.reshape(2, half)], 1)
    rows = gather(block, count)
    tokens, pairs = rows[:, :width], rows[:, width:]
    prefixes = pairs.reshape(count, width)
    owner = jnp.array(slot_masks(count), jnp.int32) ^ me
    order = (owner[:, None] * 2 + jnp.arange(2, dtype=jnp.int32)).reshape(hyp)
    perm = (order[:, None] == jnp.arange(hyp)[None, :]).astype(BF)
    flow = jnp.dot(perm, d_hidden, preferred_element_type=F32)
    match = (owner[:, None] == parent[None, :]).astype(BF)
    onehot = lax.dot_general(match, perm, (((1,), (1,)), ((), ())), preferred_element_type=F32).astype(BF)
    picked = lax.dot_general(onehot, prefixes, (((0,), (0,)), ((), ())), preferred_element_type=F32)
    inputs = (picked + tokens.astype(F32)).astype(BF)
    gate = jnp.dot(inputs, w_gate, preferred_element_type=F32)
    up = jnp.dot(inputs, w_up, preferred_element_type=F32)
    sig = jax.nn.sigmoid(gate)
    d_gate = (flow * up * sig * (1.0 + gate * (1.0 - sig))).astype(BF)
    d_up = (flow * gate * sig).astype(BF)
    parent_gate = jnp.dot(onehot, d_gate, preferred_element_type=F32).astype(BF)
    parent_up = jnp.dot(onehot, d_up, preferred_element_type=F32).astype(BF)
    contract = (((1,), (1,)), ((), ()))
    total = lax.dot_general(parent_gate, w_gate, contract, preferred_element_type=F32)
    total = total + lax.dot_general(parent_up, w_up, contract, preferred_element_type=F32)
    own = scatter(total.reshape(count * 2, half), count)
    contract = (((0,), (0,)), ((), ()))
    grad_gate = lax.dot_general(inputs, d_gate, contract, preferred_element_type=F32).astype(BF)
    grad_up = lax.dot_general(inputs, d_up, contract, preferred_element_type=F32).astype(BF)
    return grad_gate, grad_up, own.astype(BF).reshape(1, width)


def solution(mesh):
    in_specs = (
        P(("grp", "blk"), None),
        P(("grp", "blk"), None),
        P("grp"),
        P("grp", "blk"),
        P(None, "blk"),
        P(None, "blk"),
    )
    out_specs = (P(None, ("grp", "blk")), P(None, ("grp", "blk")), P(("grp", "blk"), None))
    return jax.shard_map(body, mesh=mesh, in_specs=in_specs, out_specs=out_specs, check_vma=False)
```

```python
import functools

import jax
import jax.numpy as jnp
from jax import lax
from jax.experimental import pallas as pl
from jax.experimental.pallas import tpu as pltpu
from jax.sharding import PartitionSpec as P

BF = jnp.bfloat16
F32 = jnp.float32
MIB = 1 << 20
VMEM = pl.BlockSpec(memory_space=pltpu.VMEM)
SMEM = pl.BlockSpec(memory_space=pltpu.SMEM)


def factors(count):
    chips = count // 2
    bits = chips.bit_length() - 1
    outer = 1 << ((bits + 1) // 2)
    return outer, chips // outer, 2


def send(x, mask, count):
    return lax.ppermute(x, "blk", [(i, i ^ mask) for i in range(count)])


def slot_owner(slot, me, count):
    outer, inner, _ = factors(count)
    z = slot & (outer - 1)
    rest = slot >> (outer.bit_length() - 1)
    y = rest & (inner - 1)
    core = rest >> (inner.bit_length() - 1)
    return me ^ ((z * inner + y) * 2 + core)


def pack_kernel(parent_ref, token_ref, out_ref):
    width = token_ref.shape[1]
    half = width // 2
    out_ref[:, :width] = token_ref[...]
    row = parent_ref[...].astype(F32)
    out_ref[:, width:] = jnp.concatenate([row[:, :half], row[:, half:]], 0).astype(BF)


def pack(parent_rows, token_rows):
    width = token_rows.shape[1]
    return pl.pallas_call(
        pack_kernel,
        out_shape=jax.ShapeDtypeStruct((2, width * 3 // 2), BF),
        in_specs=[VMEM] * 2,
        out_specs=VMEM,
        compiler_params=pltpu.CompilerParams(vmem_limit_bytes=4 * MIB),
        name="pack",
    )(parent_rows, token_rows)


def forward_kernel(count, columns, me_ref, parent_ref, flow_ref, wg_ref, wu_ref, *refs):
    cols, (x_ref, d_ref, own_ref, out_ref) = refs[:columns], refs[columns:]
    hyp = parent_ref.shape[1]
    width = wg_ref.shape[0]
    half = width // 2
    rows = 2 * count
    me = me_ref[0]

    line = lax.broadcasted_iota(jnp.int32, (hyp, hyp), 0)
    order = slot_owner(line >> 1, me, count) * 2 + (line & 1)
    perm = order == lax.broadcasted_iota(jnp.int32, (hyp, hyp), 1)
    flow = jnp.dot(perm.astype(F32).astype(BF), flow_ref[...], preferred_element_type=F32)
    owner = jnp.sum(jnp.where(perm, parent_ref[...].astype(F32), 0.0), axis=1, keepdims=True)
    pair = lax.broadcasted_iota(jnp.int32, (hyp, rows), 1)
    match = slot_owner(pair >> 1, me, count).astype(F32) == owner
    even = jnp.where(match & ((pair & 1) == 0), 1.0, 0.0).astype(BF)
    odd = jnp.where(match & ((pair & 1) == 1), 1.0, 0.0).astype(BF)
    pick = jnp.concatenate([even, odd], 0)

    step = min(512, half)
    acc = jnp.zeros((hyp, 256), F32)
    for at in range(0, half, step):
        here, there, held = (pl.ds(at + base, step) for base in (0, half, width))
        pairs = jnp.concatenate([c[:, held].astype(F32) for c in cols], 0).astype(BF)
        picked = jnp.dot(pick, pairs, preferred_element_type=F32)
        for base, sel in ((0, here), (half, there)):
            tokens = jnp.concatenate([c[:, sel].astype(F32) for c in cols], 0)
            top = 0 if base == 0 else hyp
            x = (picked[top:top + hyp] + tokens).astype(BF)
            x_ref[:, sel] = x
            w = jnp.concatenate([wg_ref[sel, :], wu_ref[sel, :]], 1)
            acc = acc + jnp.dot(x, w, preferred_element_type=F32)

    gate, up = acc[:, :128], acc[:, 128:]
    sig = 1.0 / (1.0 + jnp.exp(-gate))
    d_gate = (flow * up * sig * (1.0 + gate * (1.0 - sig))).astype(BF)
    d_up = (flow * gate * sig).astype(BF)
    d = jnp.concatenate([d_gate, d_up], 1)
    d_ref[...] = d
    over = (((0,), (0,)), ((), ()))
    sum_even = lax.dot_general(even, d, over, preferred_element_type=F32).astype(BF)
    sum_odd = lax.dot_general(odd, d, over, preferred_element_type=F32).astype(BF)
    back = (((1,), (1,)), ((), ()))
    for at in range(0, half, step):
        here, there = pl.ds(at, step), pl.ds(at + half, step)
        w0 = jnp.concatenate([wg_ref[here, :], wu_ref[here, :]], 1)
        w1 = jnp.concatenate([wg_ref[there, :], wu_ref[there, :]], 1)
        term = lax.dot_general(sum_even, w0, back, preferred_element_type=F32)
        term = term + lax.dot_general(sum_odd, w1, back, preferred_element_type=F32)
        own_ref[:, here] = term[:count]
        out_ref[:, here] = term[count:].astype(BF)


def forward(me, parent, d_hidden, w_gate, w_up, columns, count):
    width = w_gate.shape[0]
    hyp = parent.shape[0]
    return pl.pallas_call(
        functools.partial(forward_kernel, count, len(columns)),
        out_shape=(
            jax.ShapeDtypeStruct((hyp, width), BF),
            jax.ShapeDtypeStruct((hyp, 256), BF),
            jax.ShapeDtypeStruct((count, width // 2), F32),
            jax.ShapeDtypeStruct((count, width // 2), BF),
        ),
        in_specs=[SMEM] + [VMEM] * (4 + len(columns)),
        out_specs=(VMEM,) * 4,
        compiler_params=pltpu.CompilerParams(vmem_limit_bytes=48 * MIB if count > 16 else 24 * MIB),
        cost_estimate=pl.CostEstimate(flops=8 * hyp * width * 128, bytes_accessed=4 * width * 128, transcendentals=hyp * 128),
        name="forward",
    )(me, parent.reshape(1, hyp), d_hidden, w_gate, w_up, *columns)


def weight_kernel(x_ref, d_ref, gate_ref, up_ref):
    over = (((0,), (0,)), ((), ()))
    term = lax.dot_general(x_ref[...], d_ref[...], over, preferred_element_type=F32)
    gate_ref[...] = term[:, :128].astype(BF)
    up_ref[...] = term[:, 128:].astype(BF)


def weight_terms(x, d):
    hyp, width = x.shape
    tile = 1024
    shape = jax.ShapeDtypeStruct((width, 128), BF)
    return pl.pallas_call(
        weight_kernel,
        grid=(width // tile,),
        out_shape=(shape, shape),
        in_specs=[pl.BlockSpec((hyp, tile), lambda i: (0, i)), pl.BlockSpec((hyp, 256), lambda i: (0, 0))],
        out_specs=(pl.BlockSpec((tile, 128), lambda i: (i, 0)),) * 2,
        compiler_params=pltpu.CompilerParams(vmem_limit_bytes=16 * MIB),
        cost_estimate=pl.CostEstimate(flops=4 * hyp * width * 128, bytes_accessed=4 * width * 128, transcendentals=0),
        name="weight_terms",
    )(x, d)


def body(parent_rows, token_rows, parent, d_hidden, w_gate, w_up):
    count = lax.axis_size("blk")
    outer, inner, _ = factors(count)
    width = token_rows.shape[1]
    me = lax.axis_index("blk").reshape(1)

    block = pack(parent_rows, token_rows)
    column = jnp.concatenate([block] + [send(block, z * inner * 2, count) for z in range(1, outer)], 0)
    plane = [column] + [send(column, y * 2, count) for y in range(1, inner)]
    columns = plane + [send(c, 1, count) for c in plane]

    x, d, own, other = forward(me, parent, d_hidden, w_gate, w_up, columns, count)
    total = own + send(other, 1, count).astype(F32)
    step = outer * 2
    rows = total[:step]
    for y in range(1, inner):
        rows = rows + send(total[y * step:(y + 1) * step].astype(BF), y * 2, count).astype(F32)
    mine = rows[:2]
    for z in range(1, outer):
        mine = mine + send(rows[2 * z:2 * z + 2].astype(BF), z * inner * 2, count).astype(F32)
    grad_gate, grad_up = weight_terms(x, d)
    return grad_gate, grad_up, mine.astype(BF).reshape(1, width)


def solution(mesh):
    in_specs = (
        P(("grp", "blk"), None),
        P(("grp", "blk"), None),
        P("grp"),
        P("grp", "blk"),
        P(None, "blk"),
        P(None, "blk"),
    )
    out_specs = (P(None, ("grp", "blk")), P(None, ("grp", "blk")), P(("grp", "blk"), None))
    return jax.shard_map(body, mesh=mesh, in_specs=in_specs, out_specs=out_specs, check_vma=False)
```

```python
import functools

import jax
import jax.numpy as jnp
from jax import lax
from jax.experimental import pallas as pl
from jax.experimental.pallas import tpu as pltpu
from jax.sharding import PartitionSpec as P

BF = jnp.bfloat16
F32 = jnp.float32
MIB = 1 << 20
VMEM = pl.BlockSpec(memory_space=pltpu.VMEM)
HBM = pl.BlockSpec(memory_space=pltpu.HBM)
SMEM = pl.BlockSpec(memory_space=pltpu.SMEM)


def factors(count):
    chips = count // 2
    bits = chips.bit_length() - 1
    outer = 1 << ((bits + 1) // 2)
    return outer, chips // outer, 2


def send(x, mask, count):
    return lax.ppermute(x, "blk", [(i, i ^ mask) for i in range(count)])


def slot_owner(slot, me, count):
    outer, inner, _ = factors(count)
    z = slot & (outer - 1)
    rest = slot >> (outer.bit_length() - 1)
    y = rest & (inner - 1)
    core = rest >> (inner.bit_length() - 1)
    return me ^ ((z * inner + y) * 2 + core)


def pack_kernel(parent_ref, token_ref, out_ref, parent_buf, token_buf, sems):
    width = token_ref.shape[1]
    half = width // 2
    copies = [
        pltpu.make_async_copy(parent_ref, parent_buf, sems.at[0]),
        pltpu.make_async_copy(token_ref, token_buf, sems.at[1]),
    ]
    for copy in copies:
        copy.start()
    for copy in copies:
        copy.wait()
    out_ref[:, :width] = token_buf[...]
    row = parent_buf[...].astype(F32)
    out_ref[:, width:] = jnp.concatenate([row[:, :half], row[:, half:]], 0).astype(BF)


def pack(parent_rows, token_rows):
    width = token_rows.shape[1]
    return pl.pallas_call(
        pack_kernel,
        out_shape=jax.ShapeDtypeStruct((2, width * 3 // 2), BF),
        in_specs=[HBM] * 2,
        out_specs=VMEM,
        scratch_shapes=[
            pltpu.VMEM((1, width), BF),
            pltpu.VMEM((2, width), BF),
            pltpu.SemaphoreType.DMA((2,)),
        ],
        compiler_params=pltpu.CompilerParams(vmem_limit_bytes=48 * MIB),
        name="pack",
    )(parent_rows, token_rows)


def flip_kernel(w_ref, out_ref, flip_ref):
    out_ref[...] = w_ref[...]
    flip_ref[...] = w_ref[...].T


def flip(w):
    return pl.pallas_call(
        flip_kernel,
        out_shape=(jax.ShapeDtypeStruct(w.shape, BF), jax.ShapeDtypeStruct(w.shape[::-1], BF)),
        in_specs=[VMEM],
        out_specs=(VMEM,) * 2,
        compiler_params=pltpu.CompilerParams(vmem_limit_bytes=16 * MIB),
        cost_estimate=pl.CostEstimate(flops=0, bytes_accessed=4 * w.size, transcendentals=0),
        name="flip",
    )(w)


def select_kernel(count, me_ref, parent_ref, flow_ref, flow_out, pick_ref, sums_ref):
    hyp = parent_ref.shape[1]
    rows = 2 * count
    me = me_ref[0]
    line = lax.broadcasted_iota(jnp.int32, (hyp, hyp), 0)
    order = slot_owner(line >> 1, me, count) * 2 + (line & 1)
    perm = order == lax.broadcasted_iota(jnp.int32, (hyp, hyp), 1)
    flow_out[...] = jnp.dot(perm.astype(F32).astype(BF), flow_ref[...], preferred_element_type=F32)
    owner = jnp.sum(jnp.where(perm, parent_ref[...].astype(F32), 0.0), axis=1, keepdims=True)
    pair = lax.broadcasted_iota(jnp.int32, (hyp, rows), 1)
    match = slot_owner(pair >> 1, me, count).astype(F32) == owner
    even = jnp.where(match & ((pair & 1) == 0), 1.0, 0.0)
    odd = jnp.where(match & ((pair & 1) == 1), 1.0, 0.0)
    pick_ref[...] = jnp.concatenate([even, odd], 0).astype(BF)
    sums_ref[...] = jnp.concatenate([even.T, odd.T], 0).astype(BF)


def select(me, parent, d_hidden, count):
    hyp = parent.shape[0]
    return pl.pallas_call(
        functools.partial(select_kernel, count),
        out_shape=(
            jax.ShapeDtypeStruct(d_hidden.shape, F32),
            jax.ShapeDtypeStruct((2 * hyp, 2 * count), BF),
            jax.ShapeDtypeStruct((4 * count, hyp), BF),
        ),
        in_specs=[SMEM, VMEM, VMEM],
        out_specs=(VMEM,) * 3,
        compiler_params=pltpu.CompilerParams(vmem_limit_bytes=16 * MIB),
        name="select",
    )(me, parent.reshape(1, hyp), d_hidden)


def forward_kernel(columns, flow_ref, pick_ref, sums_ref, wg_ref, wu_ref, wgt_ref, wut_ref, *refs):
    cols, (x_ref, d_ref, own_ref, out_ref) = refs[:columns], refs[columns:]
    hyp = flow_ref.shape[0]
    width = wg_ref.shape[0]
    half = width // 2
    rows = sums_ref.shape[0] // 2
    count = rows // 2

    step = 1024
    for at in range(0, half, step):
        here, there, held = (pl.ds(at + base, step) for base in (0, half, width))
        pairs = jnp.concatenate([c[:, held].astype(F32) for c in cols], 0).astype(BF)
        picked = jnp.dot(pick_ref[...], pairs, preferred_element_type=F32)
        for top, sel in ((0, here), (hyp, there)):
            tokens = jnp.concatenate([c[:, sel].astype(F32) for c in cols], 0)
            x_ref[:, sel] = (picked[top:top + hyp] + tokens).astype(BF)

    gate = jnp.dot(x_ref[...], wg_ref[...], preferred_element_type=F32)
    up = jnp.dot(x_ref[...], wu_ref[...], preferred_element_type=F32)
    flow = flow_ref[...]
    sig = 1.0 / (1.0 + jnp.exp(-gate))
    d_gate = (flow * up * sig * (1.0 + gate * (1.0 - sig))).astype(BF)
    d_up = (flow * gate * sig).astype(BF)
    d = jnp.concatenate([d_gate, d_up], 1)
    d_ref[...] = d
    sums = jnp.dot(sums_ref[...], d, preferred_element_type=F32).astype(BF)
    for at in range(0, half, step):
        here, there = pl.ds(at, step), pl.ds(at + half, step)
        w0 = jnp.concatenate([wgt_ref[:, here], wut_ref[:, here]], 0)
        w1 = jnp.concatenate([wgt_ref[:, there], wut_ref[:, there]], 0)
        term = jnp.dot(sums[:rows], w0, preferred_element_type=F32)
        term = term + jnp.dot(sums[rows:], w1, preferred_element_type=F32)
        own_ref[:, here] = term[:count]
        out_ref[:, here] = term[count:].astype(BF)


def forward(flow, pick, sums, w_gate, w_up, flip_gate, flip_up, columns):
    width, hidden = w_gate.shape
    hyp = flow.shape[0]
    count = sums.shape[0] // 4
    return pl.pallas_call(
        functools.partial(forward_kernel, len(columns)),
        out_shape=(
            jax.ShapeDtypeStruct((hyp, width), BF),
            jax.ShapeDtypeStruct((hyp, 2 * hidden), BF),
            jax.ShapeDtypeStruct((count, width // 2), F32),
            jax.ShapeDtypeStruct((count, width // 2), BF),
        ),
        in_specs=[VMEM] * (7 + len(columns)),
        out_specs=(VMEM,) * 4,
        compiler_params=pltpu.CompilerParams(vmem_limit_bytes=48 * MIB if count > 16 else 24 * MIB),
        cost_estimate=pl.CostEstimate(flops=8 * hyp * width * hidden, bytes_accessed=8 * width * hidden, transcendentals=hyp * hidden),
        name="forward",
    )(flow, pick, sums, w_gate, w_up, flip_gate, flip_up, *columns)


def weight_kernel(step, x_ref, d_ref, gate_ref, up_ref, gate_buf, up_buf, sems):
    over = (((0,), (0,)), ((), ()))
    hidden = gate_ref.shape[1]
    copies = []
    for i in range(x_ref.shape[1] // step):
        rows = pl.ds(i * step, step)
        term = lax.dot_general(x_ref[:, rows], d_ref[...], over, preferred_element_type=F32)
        gate_buf[rows, :] = term[:, :hidden].astype(BF)
        up_buf[rows, :] = term[:, hidden:].astype(BF)
        for j, (buf, ref) in enumerate(((gate_buf, gate_ref), (up_buf, up_ref))):
            copies.append(pltpu.make_async_copy(buf.at[rows], ref.at[rows], sems.at[2 * i + j]))
            copies[-1].start()
    for copy in copies:
        copy.wait()


def weight_terms(x, d):
    hyp, width = x.shape
    hidden = d.shape[1] // 2
    step = 1024
    shape = jax.ShapeDtypeStruct((width, hidden), BF)
    return pl.pallas_call(
        functools.partial(weight_kernel, step),
        out_shape=(shape, shape),
        in_specs=[VMEM] * 2,
        out_specs=(HBM,) * 2,
        scratch_shapes=[
            pltpu.VMEM((width, hidden), BF),
            pltpu.VMEM((width, hidden), BF),
            pltpu.SemaphoreType.DMA((2 * (width // step),)),
        ],
        compiler_params=pltpu.CompilerParams(vmem_limit_bytes=24 * MIB),
        cost_estimate=pl.CostEstimate(flops=4 * hyp * width * hidden, bytes_accessed=4 * width * hidden, transcendentals=0),
        name="weight_terms",
    )(x, d)


def body(parent_rows, token_rows, parent, d_hidden, w_gate, w_up):
    count = lax.axis_size("blk")
    outer, inner, _ = factors(count)
    width = token_rows.shape[1]
    me = lax.axis_index("blk").reshape(1)

    block = pack(parent_rows, token_rows)
    column = jnp.concatenate([block] + [send(block, z * inner * 2, count) for z in range(1, outer)], 0)
    plane = [column] + [send(column, y * 2, count) for y in range(1, inner)]
    ready = (select(me, parent, d_hidden, count), flip(w_gate), flip(w_up))
    plane[-1], ready = lax.optimization_barrier((plane[-1], ready))
    columns = plane + [send(c, 1, count) for c in plane]

    (flow, pick, sums), (w_gate, flip_gate), (w_up, flip_up) = ready
    x, d, own, other = forward(flow, pick, sums, w_gate, w_up, flip_gate, flip_up, columns)
    total = own + send(other, 1, count).astype(F32)
    step = outer * 2
    rows = total[:step]
    for y in range(1, inner):
        rows = rows + send(total[y * step:(y + 1) * step].astype(BF), y * 2, count).astype(F32)
    rows, grads = lax.optimization_barrier((rows, weight_terms(x, d)))
    mine = rows[:2]
    for z in range(1, outer):
        mine = mine + send(rows[2 * z:2 * z + 2].astype(BF), z * inner * 2, count).astype(F32)
    return *grads, mine.astype(BF).reshape(1, width)


def solution(mesh):
    in_specs = (
        P(("grp", "blk"), None),
        P(("grp", "blk"), None),
        P("grp"),
        P("grp", "blk"),
        P(None, "blk"),
        P(None, "blk"),
    )
    out_specs = (P(None, ("grp", "blk")), P(None, ("grp", "blk")), P(("grp", "blk"), None))
    return jax.shard_map(body, mesh=mesh, in_specs=in_specs, out_specs=out_specs, check_vma=False)
```

```python
import functools

import jax
import jax.numpy as jnp
from jax import lax
from jax.experimental import pallas as pl
from jax.experimental.pallas import tpu as pltpu
from jax.sharding import PartitionSpec as P

BF = jnp.bfloat16
F32 = jnp.float32
MIB = 1 << 20
VMEM = pl.BlockSpec(memory_space=pltpu.VMEM)
HBM = pl.BlockSpec(memory_space=pltpu.HBM)
SMEM = pl.BlockSpec(memory_space=pltpu.SMEM)


def factors(count):
    chips = count // 2
    bits = chips.bit_length() - 1
    outer = 1 << ((bits + 1) // 2)
    return outer, chips // outer, 2


def send(x, mask, count):
    return lax.ppermute(x, "blk", [(i, i ^ mask) for i in range(count)])


def scatter_stages(count):
    outer, inner, _ = factors(count)
    z_steps = [(1 << i) * inner * 2 for i in range(outer.bit_length() - 1)]
    y_steps = [(1 << i) * 2 for i in range(inner.bit_length() - 1)]
    squares = [[0, z, y, z ^ y] for z, y in zip(z_steps, y_steps)]
    return [[0, 1]] + squares + [[0, z] for z in z_steps[len(y_steps):]]


def scatter_masks(count):
    masks = [0]
    for stage in reversed(scatter_stages(count)):
        masks = [piece ^ m for piece in stage for m in masks]
    return masks


def gather_masks(count):
    outer, inner, _ = factors(count)
    if (outer, inner) == (4, 2):
        chips = [(0, 0), (1, 0), (2, 0), (0, 1), (1, 1), (2, 1), (3, 0), (3, 1)]
        return [(z * inner + y) * 2 + c for c in range(2) for z, y in chips]
    return [(z * inner + y) * 2 + c for c in range(2) for y in range(inner) for z in range(outer)]


def gather(block, count, beside):
    outer, inner, _ = factors(count)
    to = lambda x, z, y: send(x, (z * inner + y) * 2, count)
    if (outer, inner) == (4, 2):
        far, near, side = to(block, 2, 0), to(block, 1, 0), to(block, 0, 1)
        side, near, far = lax.optimization_barrier((side, near, far))
        corner = to(side, 3, 0)
        pair = to(jnp.concatenate([near, far], 0), 0, 1)
        third = to(far, 1, 0)
        plane = [jnp.concatenate([block, near, far, side], 0), jnp.concatenate([pair, third, corner], 0)]
    else:
        column = jnp.concatenate([block] + [to(block, z, 0) for z in range(1, outer)], 0)
        plane = [column] + [to(column, 0, y) for y in range(1, inner)]
    plane[-1], beside = lax.optimization_barrier((plane[-1], beside))
    return plane + [send(p, 1, count) for p in plane], beside


def owner_of(slot, me, masks):
    mask = jnp.zeros_like(slot)
    for i, m in enumerate(masks):
        mask = jnp.where(slot == i, m, mask)
    return me ^ mask


def pack_kernel(parent_ref, token_ref, out_ref, parent_buf, token_buf, sems):
    width = token_ref.shape[1]
    half = width // 2
    copies = [
        pltpu.make_async_copy(parent_ref, parent_buf, sems.at[0]),
        pltpu.make_async_copy(token_ref, token_buf, sems.at[1]),
    ]
    for copy in copies:
        copy.start()
    for copy in copies:
        copy.wait()
    out_ref[:, :width] = token_buf[...]
    row = parent_buf[...].astype(F32)
    out_ref[:, width:] = jnp.concatenate([row[:, :half], row[:, half:]], 0).astype(BF)


def pack(parent_rows, token_rows):
    width = token_rows.shape[1]
    return pl.pallas_call(
        pack_kernel,
        out_shape=jax.ShapeDtypeStruct((2, width * 3 // 2), BF),
        in_specs=[HBM] * 2,
        out_specs=VMEM,
        scratch_shapes=[
            pltpu.VMEM((1, width), BF),
            pltpu.VMEM((2, width), BF),
            pltpu.SemaphoreType.DMA((2,)),
        ],
        compiler_params=pltpu.CompilerParams(vmem_limit_bytes=4 * MIB),
        cost_estimate=pl.CostEstimate(flops=1 << 38, bytes_accessed=1024 * MIB, transcendentals=0),
        name="pack",
    )(parent_rows, token_rows)


def flip_kernel(w_ref, out_ref, flip_ref):
    out_ref[...] = w_ref[...]
    flip_ref[...] = w_ref[...].T


def flip(w):
    return pl.pallas_call(
        flip_kernel,
        out_shape=(jax.ShapeDtypeStruct(w.shape, BF), jax.ShapeDtypeStruct(w.shape[::-1], BF)),
        in_specs=[VMEM],
        out_specs=(VMEM,) * 2,
        compiler_params=pltpu.CompilerParams(vmem_limit_bytes=16 * MIB),
        cost_estimate=pl.CostEstimate(flops=0, bytes_accessed=4 * w.size, transcendentals=0),
        name="flip",
    )(w)


def select_kernel(count, me_ref, parent_ref, flow_ref, flow_out, pick_ref, sums_ref):
    hyp = parent_ref.shape[1]
    rows = 2 * count
    me = me_ref[0]
    line = lax.broadcasted_iota(jnp.int32, (hyp, hyp), 0)
    order = owner_of(line >> 1, me, gather_masks(count)) * 2 + (line & 1)
    perm = order == lax.broadcasted_iota(jnp.int32, (hyp, hyp), 1)
    flow_out[...] = jnp.dot(perm.astype(F32).astype(BF), flow_ref[...], preferred_element_type=F32)
    owner = jnp.sum(jnp.where(perm, parent_ref[...].astype(F32), 0.0), axis=1, keepdims=True)
    pair = lax.broadcasted_iota(jnp.int32, (hyp, rows), 1)

    def halves(masks):
        match = owner_of(pair >> 1, me, masks).astype(F32) == owner
        return [jnp.where(match & ((pair & 1) == side), 1.0, 0.0) for side in (0, 1)]

    pick_ref[...] = jnp.concatenate(halves(gather_masks(count)), 0).astype(BF)
    sums_ref[...] = jnp.concatenate([h.T for h in halves(scatter_masks(count))], 0).astype(BF)


def select(me, parent, d_hidden, count):
    hyp = parent.shape[0]
    return pl.pallas_call(
        functools.partial(select_kernel, count),
        out_shape=(
            jax.ShapeDtypeStruct(d_hidden.shape, F32),
            jax.ShapeDtypeStruct((2 * hyp, 2 * count), BF),
            jax.ShapeDtypeStruct((4 * count, hyp), BF),
        ),
        in_specs=[SMEM, VMEM, VMEM],
        out_specs=(VMEM,) * 3,
        compiler_params=pltpu.CompilerParams(vmem_limit_bytes=16 * MIB),
        name="select",
    )(me, parent.reshape(1, hyp), d_hidden)


def forward_kernel(columns, flow_ref, pick_ref, sums_ref, wg_ref, wu_ref, wgt_ref, wut_ref, *refs):
    cols, (x_ref, d_ref, own_ref, out_ref) = refs[:columns], refs[columns:]
    hyp = flow_ref.shape[0]
    width = wg_ref.shape[0]
    half = width // 2
    rows = sums_ref.shape[0] // 2
    count = rows // 2

    step = 1024
    for at in range(0, half, step):
        here, there, held = (pl.ds(at + base, step) for base in (0, half, width))
        pairs = jnp.concatenate([c[:, held].astype(F32) for c in cols], 0).astype(BF)
        picked = jnp.dot(pick_ref[...], pairs, preferred_element_type=F32)
        for top, sel in ((0, here), (hyp, there)):
            tokens = jnp.concatenate([c[:, sel].astype(F32) for c in cols], 0)
            x_ref[:, sel] = (picked[top:top + hyp] + tokens).astype(BF)

    gate = jnp.dot(x_ref[...], wg_ref[...], preferred_element_type=F32)
    up = jnp.dot(x_ref[...], wu_ref[...], preferred_element_type=F32)
    flow = flow_ref[...]
    sig = 1.0 / (1.0 + jnp.exp(-gate))
    d_gate = (flow * up * sig * (1.0 + gate * (1.0 - sig))).astype(BF)
    d_up = (flow * gate * sig).astype(BF)
    d = jnp.concatenate([d_gate, d_up], 1)
    d_ref[...] = d
    sums = jnp.dot(sums_ref[...], d, preferred_element_type=F32).astype(BF)
    for at in range(0, half, step):
        here, there = pl.ds(at, step), pl.ds(at + half, step)
        w0 = jnp.concatenate([wgt_ref[:, here], wut_ref[:, here]], 0)
        w1 = jnp.concatenate([wgt_ref[:, there], wut_ref[:, there]], 0)
        term = jnp.dot(sums[:rows], w0, preferred_element_type=F32)
        term = term + jnp.dot(sums[rows:], w1, preferred_element_type=F32)
        own_ref[:, here] = term[:count]
        out_ref[:, here] = term[count:].astype(BF)


def forward(flow, pick, sums, w_gate, w_up, flip_gate, flip_up, columns):
    width, hidden = w_gate.shape
    hyp = flow.shape[0]
    count = sums.shape[0] // 4
    return pl.pallas_call(
        functools.partial(forward_kernel, len(columns)),
        out_shape=(
            jax.ShapeDtypeStruct((hyp, width), BF),
            jax.ShapeDtypeStruct((hyp, 2 * hidden), BF),
            jax.ShapeDtypeStruct((count, width // 2), F32),
            jax.ShapeDtypeStruct((count, width // 2), BF),
        ),
        in_specs=[VMEM] * (7 + len(columns)),
        out_specs=(VMEM,) * 4,
        compiler_params=pltpu.CompilerParams(vmem_limit_bytes=48 * MIB if count > 16 else 24 * MIB),
        cost_estimate=pl.CostEstimate(flops=8 * hyp * width * hidden, bytes_accessed=8 * width * hidden, transcendentals=hyp * hidden),
        name="forward",
    )(flow, pick, sums, w_gate, w_up, flip_gate, flip_up, *columns)


def weight_kernel(step, x_ref, d_ref, gate_ref, up_ref, gate_buf, up_buf, sems):
    over = (((0,), (0,)), ((), ()))
    hidden = gate_ref.shape[1]
    copies = []
    for i in range(x_ref.shape[1] // step):
        rows = pl.ds(i * step, step)
        term = lax.dot_general(x_ref[:, rows], d_ref[...], over, preferred_element_type=F32)
        gate_buf[rows, :] = term[:, :hidden].astype(BF)
        up_buf[rows, :] = term[:, hidden:].astype(BF)
        for j, (buf, ref) in enumerate(((gate_buf, gate_ref), (up_buf, up_ref))):
            copies.append(pltpu.make_async_copy(buf.at[rows], ref.at[rows], sems.at[2 * i + j]))
            copies[-1].start()
    for copy in copies:
        copy.wait()


def weight_terms(x, d):
    hyp, width = x.shape
    hidden = d.shape[1] // 2
    step = 1024
    shape = jax.ShapeDtypeStruct((width, hidden), BF)
    return pl.pallas_call(
        functools.partial(weight_kernel, step),
        out_shape=(shape, shape),
        in_specs=[VMEM] * 2,
        out_specs=(HBM,) * 2,
        scratch_shapes=[
            pltpu.VMEM((width, hidden), BF),
            pltpu.VMEM((width, hidden), BF),
            pltpu.SemaphoreType.DMA((2 * (width // step),)),
        ],
        compiler_params=pltpu.CompilerParams(vmem_limit_bytes=24 * MIB),
        cost_estimate=pl.CostEstimate(flops=4 * hyp * width * hidden, bytes_accessed=4 * width * hidden, transcendentals=0),
        name="weight_terms",
    )(x, d)


def body(parent_rows, token_rows, parent, d_hidden, w_gate, w_up):
    count = lax.axis_size("blk")
    outer, inner, _ = factors(count)
    width = token_rows.shape[1]
    me = lax.axis_index("blk").reshape(1)

    block = pack(parent_rows, token_rows)
    beside = (select(me, parent, d_hidden, count), flip(w_gate), flip(w_up))
    columns, beside = gather(block, count, beside)
    (flow, pick, sums), (w_gate, flip_gate), (w_up, flip_up) = beside
    x, d, own, other = forward(flow, pick, sums, w_gate, w_up, flip_gate, flip_up, columns)
    rows = own + send(other, 1, count).astype(F32)
    for i, stage in enumerate(scatter_stages(count)[1:]):
        size = rows.shape[0] // len(stage)
        parts = [rows[j * size:(j + 1) * size] for j in range(len(stage))]
        rows = parts[0]
        for mask, part in zip(stage[1:], parts[1:]):
            rows = rows + send(part.astype(BF), mask, count).astype(F32)
        if i == 0:
            rows, weights = lax.optimization_barrier((rows, weight_terms(x, d)))
    return *weights, rows.astype(BF).reshape(1, width)


def solution(mesh):
    in_specs = (
        P(("grp", "blk"), None),
        P(("grp", "blk"), None),
        P("grp"),
        P("grp", "blk"),
        P(None, "blk"),
        P(None, "blk"),
    )
    out_specs = (P(None, ("grp", "blk")), P(None, ("grp", "blk")), P(("grp", "blk"), None))
    return jax.shard_map(body, mesh=mesh, in_specs=in_specs, out_specs=out_specs, check_vma=False)
```

```python
import functools

import jax
import jax.numpy as jnp
from jax import lax
from jax.experimental import pallas as pl
from jax.experimental.pallas import tpu as pltpu
from jax.sharding import PartitionSpec as P

BF = jnp.bfloat16
F32 = jnp.float32
MIB = 1 << 20
VMEM = pl.BlockSpec(memory_space=pltpu.VMEM)
ANY = pl.BlockSpec(memory_space=pl.ANY)
HBM = pl.BlockSpec(memory_space=pltpu.HBM)
SMEM = pl.BlockSpec(memory_space=pltpu.SMEM)
LONG = pl.CostEstimate(flops=1 << 38, bytes_accessed=1024 * MIB, transcendentals=0)


def factors(count):
    chips = count // 2
    bits = chips.bit_length() - 1
    outer = 1 << ((bits + 1) // 2)
    return outer, chips // outer, 2


def send(x, mask, count):
    return lax.ppermute(x, "blk", [(i, i ^ mask) for i in range(count)])


def across(z, y, count):
    return (z * factors(count)[1] + y) * 2 + 1


def scatter_stages(count):
    outer, inner, _ = factors(count)
    z_steps = [1 << i for i in range(outer.bit_length() - 1)]
    y_steps = [1 << i for i in range(inner.bit_length() - 1)]
    squares = [[0, across(z, 0, count), across(0, y, count), across(z, y, count)] for z, y in zip(z_steps, y_steps)]
    return [[0, 1]] + squares + [[0, across(z, 0, count)] for z in z_steps[len(y_steps):]]


def scatter_masks(count):
    masks = [0]
    for stage in reversed(scatter_stages(count)):
        masks = [piece ^ m for piece in stage for m in masks]
    return masks


def gather_masks(count):
    outer, inner, _ = factors(count)
    if (outer, inner) == (4, 2):
        near, far, side = across(1, 0, count), across(2, 0, count), across(0, 1, count)
        plane = [0, near, far, side, side ^ near, side ^ far, near ^ far, across(3, 0, count) ^ side]
    else:
        column = [0] + [across(z, 0, count) for z in range(1, outer)]
        plane = column + [across(0, y, count) ^ m for y in range(1, inner) for m in column]
    return plane + [m ^ 1 for m in plane]


def after_kernel(*refs):
    pass


def after(arrays, deps):
    arrays, deps = tuple(arrays), tuple(jax.tree.leaves(deps))
    return pl.pallas_call(
        after_kernel,
        out_shape=tuple(jax.ShapeDtypeStruct(x.shape, x.dtype) for x in arrays),
        in_specs=[ANY] * (len(arrays) + len(deps)),
        out_specs=(ANY,) * len(arrays),
        input_output_aliases={i: i for i in range(len(arrays))},
        compiler_params=pltpu.CompilerParams(vmem_limit_bytes=MIB),
        name="after",
    )(*arrays, *deps)


def gather(block, count, beside):
    outer, inner, _ = factors(count)
    to = lambda x, z, y: send(x, across(z, y, count), count)
    if (outer, inner) == (4, 2):
        far, near, side = to(block, 2, 0), to(block, 1, 0), to(block, 0, 1)
        side, both, far = after((side, jnp.concatenate([near, far], 0), far), beside)
        corner = to(side, 3, 0)
        pair = to(both, 0, 1)
        third = to(far, 1, 0)
        plane = [jnp.concatenate([block, near, far, side], 0), jnp.concatenate([pair, third, corner], 0)]
    else:
        column = jnp.concatenate([block] + [to(block, z, 0) for z in range(1, outer)], 0)
        (column,) = after((column,), beside)
        plane = [column] + [to(column, 0, y) for y in range(1, inner)]
    return plane + [send(p, 1, count) for p in plane]


def owner_of(slot, me, masks):
    mask = jnp.zeros_like(slot)
    for i, m in enumerate(masks):
        mask = jnp.where(slot == i, m, mask)
    return me ^ mask


def lead_kernel(out_ref):
    out_ref[...] = jnp.zeros_like(out_ref)


def pack_kernel(lead_ref, parent_ref, token_ref, out_ref):
    width = token_ref.shape[1]
    half = width // 2
    out_ref[:, :width] = token_ref[...]
    row = parent_ref[...].astype(F32)
    out_ref[:, width:] = jnp.concatenate([row[:, :half], row[:, half:]], 0).astype(BF)


def pack(parent_rows, token_rows):
    width = token_rows.shape[1]
    lead = pl.pallas_call(
        lead_kernel,
        out_shape=jax.ShapeDtypeStruct((8, 128), F32),
        out_specs=VMEM,
        compiler_params=pltpu.CompilerParams(vmem_limit_bytes=4 * MIB),
        cost_estimate=LONG,
        name="lead",
    )()
    return pl.pallas_call(
        pack_kernel,
        out_shape=jax.ShapeDtypeStruct((2, width * 3 // 2), BF),
        in_specs=[VMEM] * 3,
        out_specs=VMEM,
        compiler_params=pltpu.CompilerParams(vmem_limit_bytes=4 * MIB),
        cost_estimate=LONG,
        name="pack",
    )(lead, parent_rows, token_rows)


def flip_kernel(w_ref, out_ref, flip_ref):
    out_ref[...] = w_ref[...]
    flip_ref[...] = w_ref[...].T


def flip(w):
    return pl.pallas_call(
        flip_kernel,
        out_shape=(jax.ShapeDtypeStruct(w.shape, BF), jax.ShapeDtypeStruct(w.shape[::-1], BF)),
        in_specs=[VMEM],
        out_specs=(VMEM,) * 2,
        compiler_params=pltpu.CompilerParams(vmem_limit_bytes=16 * MIB),
        cost_estimate=pl.CostEstimate(flops=0, bytes_accessed=4 * w.size, transcendentals=0),
        name="flip",
    )(w)


def select_kernel(count, me_ref, parent_ref, flow_ref, flow_out, pick_ref, sums_ref):
    hyp = parent_ref.shape[1]
    rows = 2 * count
    me = me_ref[0]
    line = lax.broadcasted_iota(jnp.int32, (hyp, hyp), 0)
    order = owner_of(line >> 1, me, gather_masks(count)) * 2 + (line & 1)
    perm = order == lax.broadcasted_iota(jnp.int32, (hyp, hyp), 1)
    flow_out[...] = jnp.dot(perm.astype(F32).astype(BF), flow_ref[...], preferred_element_type=F32)
    owner = jnp.sum(jnp.where(perm, parent_ref[...].astype(F32), 0.0), axis=1, keepdims=True)
    pair = lax.broadcasted_iota(jnp.int32, (hyp, rows), 1)

    def halves(masks):
        match = owner_of(pair >> 1, me, masks).astype(F32) == owner
        return [jnp.where(match & ((pair & 1) == side), 1.0, 0.0) for side in (0, 1)]

    pick_ref[...] = jnp.concatenate(halves(gather_masks(count)), 0).astype(BF)
    sums_ref[...] = jnp.concatenate([h.T for h in halves(scatter_masks(count))], 0).astype(BF)


def select(me, parent, d_hidden, count):
    hyp = parent.shape[0]
    return pl.pallas_call(
        functools.partial(select_kernel, count),
        out_shape=(
            jax.ShapeDtypeStruct(d_hidden.shape, F32),
            jax.ShapeDtypeStruct((2 * hyp, 2 * count), BF),
            jax.ShapeDtypeStruct((4 * count, hyp), BF),
        ),
        in_specs=[SMEM, VMEM, VMEM],
        out_specs=(VMEM,) * 3,
        compiler_params=pltpu.CompilerParams(vmem_limit_bytes=16 * MIB),
        name="select",
    )(me, parent.reshape(1, hyp), d_hidden)


def forward_kernel(columns, flow_ref, pick_ref, sums_ref, wg_ref, wu_ref, wgt_ref, wut_ref, *refs):
    cols, (x_ref, d_ref, own_ref, out_ref) = refs[:columns], refs[columns:]
    hyp = flow_ref.shape[0]
    width = wg_ref.shape[0]
    half = width // 2
    rows = sums_ref.shape[0] // 2
    count = rows // 2

    step = 1024
    for at in range(0, half, step):
        here, there, held = (pl.ds(at + base, step) for base in (0, half, width))
        pairs = jnp.concatenate([c[:, held].astype(F32) for c in cols], 0).astype(BF)
        picked = jnp.dot(pick_ref[...], pairs, preferred_element_type=F32)
        for top, sel in ((0, here), (hyp, there)):
            tokens = jnp.concatenate([c[:, sel].astype(F32) for c in cols], 0)
            x_ref[:, sel] = (picked[top:top + hyp] + tokens).astype(BF)

    gate = jnp.dot(x_ref[...], wg_ref[...], preferred_element_type=F32)
    up = jnp.dot(x_ref[...], wu_ref[...], preferred_element_type=F32)
    flow = flow_ref[...]
    sig = 1.0 / (1.0 + jnp.exp(-gate))
    d_gate = (flow * up * sig * (1.0 + gate * (1.0 - sig))).astype(BF)
    d_up = (flow * gate * sig).astype(BF)
    d = jnp.concatenate([d_gate, d_up], 1)
    d_ref[...] = d
    sums = jnp.dot(sums_ref[...], d, preferred_element_type=F32).astype(BF)
    for at in range(0, half, step):
        here, there = pl.ds(at, step), pl.ds(at + half, step)
        w0 = jnp.concatenate([wgt_ref[:, here], wut_ref[:, here]], 0)
        w1 = jnp.concatenate([wgt_ref[:, there], wut_ref[:, there]], 0)
        term = jnp.dot(sums[:rows], w0, preferred_element_type=F32)
        term = term + jnp.dot(sums[rows:], w1, preferred_element_type=F32)
        own_ref[:, here] = term[:count]
        out_ref[:, here] = term[count:].astype(BF)


def forward(flow, pick, sums, w_gate, w_up, flip_gate, flip_up, columns):
    width, hidden = w_gate.shape
    hyp = flow.shape[0]
    count = sums.shape[0] // 4
    return pl.pallas_call(
        functools.partial(forward_kernel, len(columns)),
        out_shape=(
            jax.ShapeDtypeStruct((hyp, width), BF),
            jax.ShapeDtypeStruct((hyp, 2 * hidden), BF),
            jax.ShapeDtypeStruct((count, width // 2), F32),
            jax.ShapeDtypeStruct((count, width // 2), BF),
        ),
        in_specs=[VMEM] * (7 + len(columns)),
        out_specs=(VMEM,) * 4,
        compiler_params=pltpu.CompilerParams(vmem_limit_bytes=48 * MIB if count > 16 else 24 * MIB),
        cost_estimate=pl.CostEstimate(flops=8 * hyp * width * hidden, bytes_accessed=8 * width * hidden, transcendentals=hyp * hidden),
        name="forward",
    )(flow, pick, sums, w_gate, w_up, flip_gate, flip_up, *columns)


def weight_kernel(step, x_ref, d_ref, gate_ref, up_ref, gate_buf, up_buf, sems):
    over = (((0,), (0,)), ((), ()))
    hidden = gate_ref.shape[1]
    copies = []
    for i in range(x_ref.shape[1] // step):
        rows = pl.ds(i * step, step)
        term = lax.dot_general(x_ref[:, rows], d_ref[...], over, preferred_element_type=F32)
        gate_buf[rows, :] = term[:, :hidden].astype(BF)
        up_buf[rows, :] = term[:, hidden:].astype(BF)
        for j, (buf, ref) in enumerate(((gate_buf, gate_ref), (up_buf, up_ref))):
            copies.append(pltpu.make_async_copy(buf.at[rows], ref.at[rows], sems.at[2 * i + j]))
            copies[-1].start()
    for copy in copies:
        copy.wait()


def weight_terms(x, d):
    hyp, width = x.shape
    hidden = d.shape[1] // 2
    step = 1024
    shape = jax.ShapeDtypeStruct((width, hidden), BF)
    return pl.pallas_call(
        functools.partial(weight_kernel, step),
        out_shape=(shape, shape),
        in_specs=[VMEM] * 2,
        out_specs=(HBM,) * 2,
        scratch_shapes=[
            pltpu.VMEM((width, hidden), BF),
            pltpu.VMEM((width, hidden), BF),
            pltpu.SemaphoreType.DMA((2 * (width // step),)),
        ],
        compiler_params=pltpu.CompilerParams(vmem_limit_bytes=24 * MIB),
        cost_estimate=pl.CostEstimate(flops=4 * hyp * width * hidden, bytes_accessed=4 * width * hidden, transcendentals=0),
        name="weight_terms",
    )(x, d)


def body(parent_rows, token_rows, parent, d_hidden, w_gate, w_up):
    count = lax.axis_size("blk")
    outer, inner, _ = factors(count)
    width = token_rows.shape[1]
    me = lax.axis_index("blk").reshape(1)

    block = pack(parent_rows, token_rows)
    beside = (select(me, parent, d_hidden, count), flip(w_gate), flip(w_up))
    columns = gather(block, count, beside)
    (flow, pick, sums), (w_gate, flip_gate), (w_up, flip_up) = beside
    x, d, own, other = forward(flow, pick, sums, w_gate, w_up, flip_gate, flip_up, columns)
    rows = own + send(other, 1, count).astype(F32)
    for i, stage in enumerate(scatter_stages(count)[1:]):
        size = rows.shape[0] // len(stage)
        parts = [rows[j * size:(j + 1) * size] for j in range(len(stage))]
        rows = parts[0]
        for mask, part in zip(stage[1:], parts[1:]):
            rows = rows + send(part.astype(BF), mask, count).astype(F32)
        if i == 0:
            rows, weights = lax.optimization_barrier((rows, weight_terms(x, d)))
    return *weights, rows.astype(BF).reshape(1, width)


def solution(mesh):
    in_specs = (
        P(("grp", "blk"), None),
        P(("grp", "blk"), None),
        P("grp"),
        P("grp", "blk"),
        P(None, "blk"),
        P(None, "blk"),
    )
    out_specs = (P(None, ("grp", "blk")), P(None, ("grp", "blk")), P(("grp", "blk"), None))
    return jax.shard_map(body, mesh=mesh, in_specs=in_specs, out_specs=out_specs, check_vma=False)
```

```python
import functools

import jax
import jax.numpy as jnp
from jax import lax
from jax.experimental import pallas as pl
from jax.experimental.pallas import tpu as pltpu
from jax.sharding import PartitionSpec as P

BF = jnp.bfloat16
F32 = jnp.float32
MIB = 1 << 20
VMEM = pl.BlockSpec(memory_space=pltpu.VMEM)
ANY = pl.BlockSpec(memory_space=pl.ANY)
HBM = pl.BlockSpec(memory_space=pltpu.HBM)
SMEM = pl.BlockSpec(memory_space=pltpu.SMEM)
LONG = pl.CostEstimate(flops=1 << 38, bytes_accessed=1024 * MIB, transcendentals=0)


def factors(count):
    chips = count // 2
    bits = chips.bit_length() - 1
    outer = 1 << ((bits + 1) // 2)
    return outer, chips // outer, 2


def send(x, mask, count):
    return lax.ppermute(x, "blk", [(i, i ^ mask) for i in range(count)])


def across(z, y, count):
    return (z * factors(count)[1] + y) * 2 + 1


def scatter_stages(count):
    outer, inner, _ = factors(count)
    z_steps = [1 << i for i in range(outer.bit_length() - 1)]
    y_steps = [1 << i for i in range(inner.bit_length() - 1)]
    squares = [[0, across(z, 0, count), across(0, y, count), across(z, y, count)] for z, y in zip(z_steps, y_steps)]
    return [[0, 1]] + squares + [[0, across(z, 0, count)] for z in z_steps[len(y_steps):]]


def scatter_masks(count):
    masks = [0]
    for stage in reversed(scatter_stages(count)):
        masks = [piece ^ m for piece in stage for m in masks]
    return masks


def gather_masks(count):
    outer, inner, _ = factors(count)
    if (outer, inner) == (4, 2):
        near, far, side = across(1, 0, count), across(2, 0, count), across(0, 1, count)
        plane = [0, near, far, side, near ^ far, across(3, 0, count) ^ side, side ^ near, side ^ far]
    else:
        column = [0] + [across(z, 0, count) for z in range(1, outer)]
        plane = column + [across(0, y, count) ^ m for y in range(1, inner) for m in column]
    return plane + [m ^ 1 for m in plane]


def after_kernel(*refs):
    pass


def after(arrays, deps):
    arrays, deps = tuple(arrays), tuple(jax.tree.leaves(deps))
    return pl.pallas_call(
        after_kernel,
        out_shape=tuple(jax.ShapeDtypeStruct(x.shape, x.dtype) for x in arrays),
        in_specs=[ANY] * (len(arrays) + len(deps)),
        out_specs=(ANY,) * len(arrays),
        input_output_aliases={i: i for i in range(len(arrays))},
        compiler_params=pltpu.CompilerParams(vmem_limit_bytes=MIB),
        name="after",
    )(*arrays, *deps)


def gather(block, count, beside):
    outer, inner, _ = factors(count)
    to = lambda x, z, y: send(x, across(z, y, count), count)
    if (outer, inner) == (4, 2):
        far, near, side = to(block, 2, 0), to(block, 1, 0), to(block, 0, 1)
        side, both, far = after((side, jnp.concatenate([near, far], 0), far), beside)
        corner = to(side, 3, 0)
        pair = to(both, 0, 1)
        third = to(far, 1, 0)
        plane = [jnp.concatenate([block, both, side], 0), jnp.concatenate([third, corner], 0), pair]
    else:
        column = jnp.concatenate([block] + [to(block, z, 0) for z in range(1, outer)], 0)
        (column,) = after((column,), beside)
        plane = [column] + [to(column, 0, y) for y in range(1, inner)]
    return plane + [send(p, 1, count) for p in plane]


def owner_of(slot, me, masks):
    mask = jnp.zeros_like(slot)
    for i, m in enumerate(masks):
        mask = jnp.where(slot == i, m, mask)
    return me ^ mask


def lead_kernel(out_ref):
    out_ref[...] = jnp.zeros_like(out_ref)


def pack_kernel(lead_ref, parent_ref, token_ref, out_ref):
    width = token_ref.shape[1]
    half = width // 2
    out_ref[:, :width] = token_ref[...]
    row = parent_ref[...].astype(F32)
    out_ref[:, width:] = jnp.concatenate([row[:, :half], row[:, half:]], 0).astype(BF)


def pack(parent_rows, token_rows):
    width = token_rows.shape[1]
    lead = pl.pallas_call(
        lead_kernel,
        out_shape=jax.ShapeDtypeStruct((8, 128), F32),
        out_specs=VMEM,
        compiler_params=pltpu.CompilerParams(vmem_limit_bytes=4 * MIB),
        cost_estimate=LONG,
        name="lead",
    )()
    return pl.pallas_call(
        pack_kernel,
        out_shape=jax.ShapeDtypeStruct((2, width * 3 // 2), BF),
        in_specs=[VMEM] * 3,
        out_specs=VMEM,
        compiler_params=pltpu.CompilerParams(vmem_limit_bytes=4 * MIB),
        cost_estimate=LONG,
        name="pack",
    )(lead, parent_rows, token_rows)


def flip_kernel(w_ref, out_ref, flip_ref):
    out_ref[...] = w_ref[...]
    flip_ref[...] = w_ref[...].T


def flip(w):
    return pl.pallas_call(
        flip_kernel,
        out_shape=(jax.ShapeDtypeStruct(w.shape, BF), jax.ShapeDtypeStruct(w.shape[::-1], BF)),
        in_specs=[VMEM],
        out_specs=(VMEM,) * 2,
        compiler_params=pltpu.CompilerParams(vmem_limit_bytes=16 * MIB),
        cost_estimate=pl.CostEstimate(flops=0, bytes_accessed=4 * w.size, transcendentals=0),
        name="flip",
    )(w)


def select_kernel(count, me_ref, parent_ref, flow_ref, flow_out, pick_ref, sums_ref):
    hyp = parent_ref.shape[1]
    rows = 2 * count
    me = me_ref[0]
    line = lax.broadcasted_iota(jnp.int32, (hyp, hyp), 0)
    order = owner_of(line >> 1, me, gather_masks(count)) * 2 + (line & 1)
    perm = order == lax.broadcasted_iota(jnp.int32, (hyp, hyp), 1)
    flow_out[...] = jnp.dot(perm.astype(F32).astype(BF), flow_ref[...], preferred_element_type=F32)
    owner = jnp.sum(jnp.where(perm, parent_ref[...].astype(F32), 0.0), axis=1, keepdims=True)
    pair = lax.broadcasted_iota(jnp.int32, (hyp, rows), 1)

    def halves(masks):
        match = owner_of(pair >> 1, me, masks).astype(F32) == owner
        return [jnp.where(match & ((pair & 1) == side), 1.0, 0.0) for side in (0, 1)]

    pick_ref[...] = jnp.concatenate(halves(gather_masks(count)), 0).astype(BF)
    sums_ref[...] = jnp.concatenate([h.T for h in halves(scatter_masks(count))], 0).astype(BF)


def select(me, parent, d_hidden, count):
    hyp = parent.shape[0]
    return pl.pallas_call(
        functools.partial(select_kernel, count),
        out_shape=(
            jax.ShapeDtypeStruct(d_hidden.shape, F32),
            jax.ShapeDtypeStruct((2 * hyp, 2 * count), BF),
            jax.ShapeDtypeStruct((4 * count, hyp), BF),
        ),
        in_specs=[SMEM, VMEM, VMEM],
        out_specs=(VMEM,) * 3,
        compiler_params=pltpu.CompilerParams(vmem_limit_bytes=16 * MIB),
        name="select",
    )(me, parent.reshape(1, hyp), d_hidden)


def forward_kernel(columns, flow_ref, pick_ref, sums_ref, wg_ref, wu_ref, wgt_ref, wut_ref, *refs):
    cols, (x_ref, d_ref, own_ref, out_ref) = refs[:columns], refs[columns:]
    hyp = flow_ref.shape[0]
    width = wg_ref.shape[0]
    half = width // 2
    rows = sums_ref.shape[0] // 2
    count = rows // 2

    step = 1024
    for at in range(0, half, step):
        here, there, held = (pl.ds(at + base, step) for base in (0, half, width))
        pairs = jnp.concatenate([c[:, held].astype(F32) for c in cols], 0).astype(BF)
        picked = jnp.dot(pick_ref[...], pairs, preferred_element_type=F32)
        for top, sel in ((0, here), (hyp, there)):
            tokens = jnp.concatenate([c[:, sel].astype(F32) for c in cols], 0)
            x_ref[:, sel] = (picked[top:top + hyp] + tokens).astype(BF)

    gate = jnp.dot(x_ref[...], wg_ref[...], preferred_element_type=F32)
    up = jnp.dot(x_ref[...], wu_ref[...], preferred_element_type=F32)
    flow = flow_ref[...]
    sig = 1.0 / (1.0 + jnp.exp(-gate))
    d_gate = (flow * up * sig * (1.0 + gate * (1.0 - sig))).astype(BF)
    d_up = (flow * gate * sig).astype(BF)
    d = jnp.concatenate([d_gate, d_up], 1)
    d_ref[...] = d
    sums = jnp.dot(sums_ref[...], d, preferred_element_type=F32).astype(BF)
    for at in range(0, half, step):
        here, there = pl.ds(at, step), pl.ds(at + half, step)
        w0 = jnp.concatenate([wgt_ref[:, here], wut_ref[:, here]], 0)
        w1 = jnp.concatenate([wgt_ref[:, there], wut_ref[:, there]], 0)
        term = jnp.dot(sums[:rows], w0, preferred_element_type=F32)
        term = term + jnp.dot(sums[rows:], w1, preferred_element_type=F32)
        own_ref[:, here] = term[:count]
        out_ref[:, here] = term[count:].astype(BF)


def forward(flow, pick, sums, w_gate, w_up, flip_gate, flip_up, columns):
    width, hidden = w_gate.shape
    hyp = flow.shape[0]
    count = sums.shape[0] // 4
    return pl.pallas_call(
        functools.partial(forward_kernel, len(columns)),
        out_shape=(
            jax.ShapeDtypeStruct((hyp, width), BF),
            jax.ShapeDtypeStruct((hyp, 2 * hidden), BF),
            jax.ShapeDtypeStruct((count, width // 2), F32),
            jax.ShapeDtypeStruct((count, width // 2), BF),
        ),
        in_specs=[VMEM] * (7 + len(columns)),
        out_specs=(VMEM,) * 4,
        compiler_params=pltpu.CompilerParams(vmem_limit_bytes=48 * MIB if count > 16 else 24 * MIB),
        cost_estimate=pl.CostEstimate(flops=8 * hyp * width * hidden, bytes_accessed=8 * width * hidden, transcendentals=hyp * hidden),
        name="forward",
    )(flow, pick, sums, w_gate, w_up, flip_gate, flip_up, *columns)


def weight_kernel(step, x_ref, d_ref, gate_ref, up_ref, gate_buf, up_buf, sems):
    over = (((0,), (0,)), ((), ()))
    hidden = gate_ref.shape[1]
    copies = []
    for i in range(x_ref.shape[1] // step):
        rows = pl.ds(i * step, step)
        term = lax.dot_general(x_ref[:, rows], d_ref[...], over, preferred_element_type=F32)
        gate_buf[rows, :] = term[:, :hidden].astype(BF)
        up_buf[rows, :] = term[:, hidden:].astype(BF)
        for j, (buf, ref) in enumerate(((gate_buf, gate_ref), (up_buf, up_ref))):
            copies.append(pltpu.make_async_copy(buf.at[rows], ref.at[rows], sems.at[2 * i + j]))
            copies[-1].start()
    for copy in copies:
        copy.wait()


def weight_terms(x, d):
    hyp, width = x.shape
    hidden = d.shape[1] // 2
    step = 1024
    shape = jax.ShapeDtypeStruct((width, hidden), BF)
    return pl.pallas_call(
        functools.partial(weight_kernel, step),
        out_shape=(shape, shape),
        in_specs=[VMEM] * 2,
        out_specs=(HBM,) * 2,
        scratch_shapes=[
            pltpu.VMEM((width, hidden), BF),
            pltpu.VMEM((width, hidden), BF),
            pltpu.SemaphoreType.DMA((2 * (width // step),)),
        ],
        compiler_params=pltpu.CompilerParams(vmem_limit_bytes=24 * MIB),
        cost_estimate=pl.CostEstimate(flops=4 * hyp * width * hidden, bytes_accessed=4 * width * hidden, transcendentals=0),
        name="weight_terms",
    )(x, d)


def body(parent_rows, token_rows, parent, d_hidden, w_gate, w_up):
    count = lax.axis_size("blk")
    outer, inner, _ = factors(count)
    width = token_rows.shape[1]
    me = lax.axis_index("blk").reshape(1)

    block = pack(parent_rows, token_rows)
    beside = (select(me, parent, d_hidden, count), flip(w_gate), flip(w_up))
    columns = gather(block, count, beside)
    (flow, pick, sums), (w_gate, flip_gate), (w_up, flip_up) = beside
    x, d, own, other = forward(flow, pick, sums, w_gate, w_up, flip_gate, flip_up, columns)
    rows = own + send(other, 1, count).astype(F32)
    for i, stage in enumerate(scatter_stages(count)[1:]):
        size = rows.shape[0] // len(stage)
        parts = [rows[j * size:(j + 1) * size] for j in range(len(stage))]
        rows = parts[0]
        for mask, part in zip(stage[1:], parts[1:]):
            rows = rows + send(part.astype(BF), mask, count).astype(F32)
        if i == 0:
            rows, weights = lax.optimization_barrier((rows, weight_terms(x, d)))
    return *weights, rows.astype(BF).reshape(1, width)


def solution(mesh):
    in_specs = (
        P(("grp", "blk"), None),
        P(("grp", "blk"), None),
        P("grp"),
        P("grp", "blk"),
        P(None, "blk"),
        P(None, "blk"),
    )
    out_specs = (P(None, ("grp", "blk")), P(None, ("grp", "blk")), P(("grp", "blk"), None))
    return jax.shard_map(body, mesh=mesh, in_specs=in_specs, out_specs=out_specs, check_vma=False)
```

```python
import functools

import jax
import jax.numpy as jnp
from jax import lax
from jax.experimental import pallas as pl
from jax.experimental.pallas import tpu as pltpu
from jax.sharding import PartitionSpec as P

BF = jnp.bfloat16
F32 = jnp.float32
MIB = 1 << 20
VMEM = pl.BlockSpec(memory_space=pltpu.VMEM)
ANY = pl.BlockSpec(memory_space=pl.ANY)
HBM = pl.BlockSpec(memory_space=pltpu.HBM)
SMEM = pl.BlockSpec(memory_space=pltpu.SMEM)
LONG = pl.CostEstimate(flops=1 << 38, bytes_accessed=1024 * MIB, transcendentals=0)


def factors(count):
    chips = count // 2
    bits = chips.bit_length() - 1
    outer = 1 << ((bits + 1) // 2)
    return outer, chips // outer, 2


def send(x, mask, count):
    return lax.ppermute(x, "blk", [(i, i ^ mask) for i in range(count)])


def across(z, y, count):
    return (z * factors(count)[1] + y) * 2 + 1


def scatter_stages(count):
    outer, inner, _ = factors(count)
    z_steps = [1 << i for i in range(outer.bit_length() - 1)]
    y_steps = [1 << i for i in range(inner.bit_length() - 1)]
    squares = [[0, across(0, y, count), across(z, 0, count), across(z, y, count)] for z, y in zip(z_steps, y_steps)]
    return [[0, 1]] + squares + [[0, across(z, 0, count)] for z in z_steps[len(y_steps):]]


def scatter_masks(count):
    masks = [0]
    for stage in reversed(scatter_stages(count)):
        masks = [piece ^ m for piece in stage for m in masks]
    return masks


def gather_masks(count):
    outer, inner, _ = factors(count)
    if (outer, inner) == (4, 2):
        near, far, side = across(1, 0, count), across(2, 0, count), across(0, 1, count)
        plane = [0, near, far, side, near ^ far, across(3, 0, count) ^ side, side ^ near, side ^ far]
    else:
        column = [0] + [across(z, 0, count) for z in range(1, outer)]
        plane = column + [across(0, y, count) ^ m for y in range(1, inner) for m in column]
    return plane + [m ^ 1 for m in plane]


def after_kernel(*refs):
    pass


def after(arrays, deps):
    arrays, deps = tuple(arrays), tuple(jax.tree.leaves(deps))
    return pl.pallas_call(
        after_kernel,
        out_shape=tuple(jax.ShapeDtypeStruct(x.shape, x.dtype) for x in arrays),
        in_specs=[ANY] * (len(arrays) + len(deps)),
        out_specs=(ANY,) * len(arrays),
        input_output_aliases={i: i for i in range(len(arrays))},
        compiler_params=pltpu.CompilerParams(vmem_limit_bytes=MIB),
        name="after",
    )(*arrays, *deps)


def gather(block, count, beside):
    outer, inner, _ = factors(count)
    to = lambda x, z, y: send(x, across(z, y, count), count)
    if (outer, inner) == (4, 2):
        far, near, side = to(block, 2, 0), to(block, 1, 0), to(block, 0, 1)
        side, both, far = after((side, jnp.concatenate([near, far], 0), far), beside)
        corner = to(side, 3, 0)
        pair = to(both, 0, 1)
        third = to(far, 1, 0)
        plane = [jnp.concatenate([block, both, side], 0), jnp.concatenate([third, corner], 0), pair]
    else:
        column = jnp.concatenate([block] + [to(block, z, 0) for z in range(1, outer)], 0)
        (column,) = after((column,), beside)
        plane = [column] + [to(column, 0, y) for y in range(1, inner)]
    return plane + [send(p, 1, count) for p in plane]


def owner_of(slot, me, masks):
    mask = jnp.zeros_like(slot)
    for i, m in enumerate(masks):
        mask = jnp.where(slot == i, m, mask)
    return me ^ mask


def lead_kernel(out_ref):
    out_ref[...] = jnp.zeros_like(out_ref)


def pack_kernel(lead_ref, parent_ref, token_ref, out_ref):
    width = token_ref.shape[1]
    half = width // 2
    out_ref[:, :width] = token_ref[...]
    row = parent_ref[...].astype(F32)
    out_ref[:, width:] = jnp.concatenate([row[:, :half], row[:, half:]], 0).astype(BF)


def pack(parent_rows, token_rows):
    width = token_rows.shape[1]
    lead = pl.pallas_call(
        lead_kernel,
        out_shape=jax.ShapeDtypeStruct((8, 128), F32),
        out_specs=VMEM,
        compiler_params=pltpu.CompilerParams(vmem_limit_bytes=4 * MIB),
        cost_estimate=LONG,
        name="lead",
    )()
    return pl.pallas_call(
        pack_kernel,
        out_shape=jax.ShapeDtypeStruct((2, width * 3 // 2), BF),
        in_specs=[VMEM] * 3,
        out_specs=VMEM,
        compiler_params=pltpu.CompilerParams(vmem_limit_bytes=4 * MIB),
        cost_estimate=LONG,
        name="pack",
    )(lead, parent_rows, token_rows)


def flip_kernel(w_ref, out_ref, flip_ref):
    out_ref[...] = w_ref[...]
    flip_ref[...] = w_ref[...].T


def flip(w):
    return pl.pallas_call(
        flip_kernel,
        out_shape=(jax.ShapeDtypeStruct(w.shape, BF), jax.ShapeDtypeStruct(w.shape[::-1], BF)),
        in_specs=[VMEM],
        out_specs=(VMEM,) * 2,
        compiler_params=pltpu.CompilerParams(vmem_limit_bytes=16 * MIB),
        cost_estimate=pl.CostEstimate(flops=0, bytes_accessed=4 * w.size, transcendentals=0),
        name="flip",
    )(w)


def select_kernel(count, me_ref, parent_ref, flow_ref, flow_out, pick_ref, sums_ref):
    hyp = parent_ref.shape[1]
    rows = 2 * count
    me = me_ref[0]
    line = lax.broadcasted_iota(jnp.int32, (hyp, hyp), 0)
    order = owner_of(line >> 1, me, gather_masks(count)) * 2 + (line & 1)
    perm = order == lax.broadcasted_iota(jnp.int32, (hyp, hyp), 1)
    flow_out[...] = jnp.dot(perm.astype(F32).astype(BF), flow_ref[...], preferred_element_type=F32)
    owner = jnp.sum(jnp.where(perm, parent_ref[...].astype(F32), 0.0), axis=1, keepdims=True)
    pair = lax.broadcasted_iota(jnp.int32, (hyp, rows), 1)

    def halves(masks):
        match = owner_of(pair >> 1, me, masks).astype(F32) == owner
        return [jnp.where(match & ((pair & 1) == side), 1.0, 0.0) for side in (0, 1)]

    pick_ref[...] = jnp.concatenate(halves(gather_masks(count)), 0).astype(BF)
    sums_ref[...] = jnp.concatenate([h.T for h in halves(scatter_masks(count))], 0).astype(BF)


def select(me, parent, d_hidden, count):
    hyp = parent.shape[0]
    return pl.pallas_call(
        functools.partial(select_kernel, count),
        out_shape=(
            jax.ShapeDtypeStruct(d_hidden.shape, F32),
            jax.ShapeDtypeStruct((2 * hyp, 2 * count), BF),
            jax.ShapeDtypeStruct((4 * count, hyp), BF),
        ),
        in_specs=[SMEM, VMEM, VMEM],
        out_specs=(VMEM,) * 3,
        compiler_params=pltpu.CompilerParams(vmem_limit_bytes=16 * MIB),
        name="select",
    )(me, parent.reshape(1, hyp), d_hidden)


def forward_kernel(columns, flow_ref, pick_ref, sums_ref, wg_ref, wu_ref, wgt_ref, wut_ref, *refs):
    cols, (x_ref, d_ref, own_ref, out_ref) = refs[:columns], refs[columns:]
    hyp = flow_ref.shape[0]
    width, hidden = wg_ref.shape
    half = width // 2
    rows = sums_ref.shape[0] // 2
    count = rows // 2

    step = 1024
    for at in range(0, half, step):
        here, there, held = (pl.ds(at + base, step) for base in (0, half, width))
        pairs = jnp.concatenate([c[:, held].astype(F32) for c in cols], 0).astype(BF)
        picked = jnp.dot(pick_ref[...], pairs, preferred_element_type=F32)
        for top, sel in ((0, here), (hyp, there)):
            tokens = jnp.concatenate([c[:, sel].astype(F32) for c in cols], 0)
            x_ref[:, sel] = (picked[top:top + hyp] + tokens).astype(BF)

    gate = jnp.dot(x_ref[...], wg_ref[...], preferred_element_type=F32)
    up = jnp.dot(x_ref[...], wu_ref[...], preferred_element_type=F32)
    flow = flow_ref[...]
    sig = 1.0 / (1.0 + jnp.exp(-gate))
    d_gate = (flow * up * sig * (1.0 + gate * (1.0 - sig))).astype(BF)
    d_up = (flow * gate * sig).astype(BF)
    d = jnp.concatenate([d_gate, d_up], 1)
    d_ref[...] = d
    sums = jnp.dot(sums_ref[...], d, preferred_element_type=F32).astype(BF)
    even, odd = sums[:rows], sums[rows:]
    for at in range(0, half, step):
        here, there = pl.ds(at, step), pl.ds(at + half, step)
        term = jnp.dot(even[:, :hidden], wgt_ref[:, here], preferred_element_type=F32)
        term = term + jnp.dot(even[:, hidden:], wut_ref[:, here], preferred_element_type=F32)
        term = term + jnp.dot(odd[:, :hidden], wgt_ref[:, there], preferred_element_type=F32)
        term = term + jnp.dot(odd[:, hidden:], wut_ref[:, there], preferred_element_type=F32)
        own_ref[:, here] = term[:count]
        out_ref[:, here] = term[count:].astype(BF)


def forward(flow, pick, sums, w_gate, w_up, flip_gate, flip_up, columns):
    width, hidden = w_gate.shape
    hyp = flow.shape[0]
    count = sums.shape[0] // 4
    return pl.pallas_call(
        functools.partial(forward_kernel, len(columns)),
        out_shape=(
            jax.ShapeDtypeStruct((hyp, width), BF),
            jax.ShapeDtypeStruct((hyp, 2 * hidden), BF),
            jax.ShapeDtypeStruct((count, width // 2), F32),
            jax.ShapeDtypeStruct((count, width // 2), BF),
        ),
        in_specs=[VMEM] * (7 + len(columns)),
        out_specs=(VMEM,) * 4,
        compiler_params=pltpu.CompilerParams(vmem_limit_bytes=48 * MIB if count > 16 else 24 * MIB),
        cost_estimate=pl.CostEstimate(flops=8 * hyp * width * hidden, bytes_accessed=8 * width * hidden, transcendentals=hyp * hidden),
        name="forward",
    )(flow, pick, sums, w_gate, w_up, flip_gate, flip_up, *columns)


def weight_kernel(side, step, x_ref, d_ref, *refs):
    out_ref, done_ref, buf, sems = refs[-4:]
    over = (((0,), (0,)), ((), ()))
    hidden = out_ref.shape[1]
    copies = []
    for i in range(x_ref.shape[1] // step):
        rows = pl.ds(i * step, step)
        d = d_ref[:, side * hidden:(side + 1) * hidden]
        buf[rows, :] = lax.dot_general(x_ref[:, rows], d, over, preferred_element_type=F32).astype(BF)
        copies.append(pltpu.make_async_copy(buf.at[rows], out_ref.at[rows], sems.at[i]))
        copies[-1].start()
    done_ref[...] = jnp.zeros_like(done_ref)
    for copy in copies:
        copy.wait()


def weight_terms(x, d, side, *deps):
    hyp, width = x.shape
    hidden = d.shape[1] // 2
    step = 1024
    return pl.pallas_call(
        functools.partial(weight_kernel, side, step),
        out_shape=(jax.ShapeDtypeStruct((width, hidden), BF), jax.ShapeDtypeStruct((8, 128), F32)),
        in_specs=[VMEM] * 2 + [ANY] * len(deps),
        out_specs=(HBM, VMEM),
        scratch_shapes=[pltpu.VMEM((width, hidden), BF), pltpu.SemaphoreType.DMA((width // step,))],
        compiler_params=pltpu.CompilerParams(vmem_limit_bytes=24 * MIB),
        cost_estimate=pl.CostEstimate(flops=2 * hyp * width * hidden, bytes_accessed=2 * width * hidden, transcendentals=0),
        name="weight_terms",
    )(x, d, *deps)


def body(parent_rows, token_rows, parent, d_hidden, w_gate, w_up):
    count = lax.axis_size("blk")
    outer, inner, _ = factors(count)
    width = token_rows.shape[1]
    me = lax.axis_index("blk").reshape(1)

    block = pack(parent_rows, token_rows)
    beside = (select(me, parent, d_hidden, count), flip(w_gate), flip(w_up))
    columns = gather(block, count, beside)
    (flow, pick, sums), (w_gate, flip_gate), (w_up, flip_up) = beside
    x, d, own, other = forward(flow, pick, sums, w_gate, w_up, flip_gate, flip_up, columns)
    rows = own + send(other, 1, count).astype(F32)
    grad_gate, done = weight_terms(x, d, 0)
    stages = scatter_stages(count)[1:]
    for i, stage in enumerate(stages):
        size = rows.shape[0] // len(stage)
        parts = [rows[j * size:(j + 1) * size] for j in range(len(stage))]
        outgoing = [part.astype(BF) for part in parts[1:]]
        if i == len(stages) - 1:
            outgoing = after(outgoing, done)
            grad_up, done = weight_terms(x, d, 1, outgoing[0])
        arrived = [send(part, mask, count) for mask, part in zip(stage[1:], outgoing)]
        if i == len(stages) - 1:
            arrived = after(arrived, done)
        rows = parts[0]
        for part in arrived:
            rows = rows + part.astype(F32)
    return grad_gate, grad_up, rows.astype(BF).reshape(1, width)


def solution(mesh):
    in_specs = (
        P(("grp", "blk"), None),
        P(("grp", "blk"), None),
        P("grp"),
        P("grp", "blk"),
        P(None, "blk"),
        P(None, "blk"),
    )
    out_specs = (P(None, ("grp", "blk")), P(None, ("grp", "blk")), P(("grp", "blk"), None))
    return jax.shard_map(body, mesh=mesh, in_specs=in_specs, out_specs=out_specs, check_vma=False)
```

```python
import functools

import jax
import jax.numpy as jnp
from jax import lax
from jax.experimental import pallas as pl
from jax.experimental.pallas import tpu as pltpu
from jax.sharding import PartitionSpec as P

BF = jnp.bfloat16
F32 = jnp.float32
MIB = 1 << 20
VMEM = pl.BlockSpec(memory_space=pltpu.VMEM)
ANY = pl.BlockSpec(memory_space=pl.ANY)
HBM = pl.BlockSpec(memory_space=pltpu.HBM)
SMEM = pl.BlockSpec(memory_space=pltpu.SMEM)
LONG = pl.CostEstimate(flops=1 << 38, bytes_accessed=1024 * MIB, transcendentals=0)


def factors(count):
    chips = count // 2
    bits = chips.bit_length() - 1
    outer = 1 << ((bits + 1) // 2)
    return outer, chips // outer, 2


def send(x, mask, count):
    return lax.ppermute(x, "blk", [(i, i ^ mask) for i in range(count)])


def across(z, y, count):
    return (z * factors(count)[1] + y) * 2 + 1


def scatter_stages(count):
    outer, inner, _ = factors(count)
    z_steps = [1 << i for i in range(outer.bit_length() - 1)]
    y_steps = [1 << i for i in range(inner.bit_length() - 1)]
    squares = [[0, across(z, y, count), across(0, y, count), across(z, 0, count)] for z, y in zip(z_steps, y_steps)]
    return [[0, 1]] + squares + [[0, across(z, 0, count)] for z in z_steps[len(y_steps):]]


def scatter_masks(count):
    masks = [0]
    for stage in reversed(scatter_stages(count)):
        masks = [piece ^ m for piece in stage for m in masks]
    return masks


def gather_masks(count):
    outer, inner, _ = factors(count)
    if (outer, inner) == (4, 2):
        near, far, side = across(1, 0, count), across(2, 0, count), across(0, 1, count)
        plane = [0, near, far, side, near ^ far, across(3, 0, count) ^ side, side ^ near, side ^ far]
    else:
        column = [0] + [across(z, 0, count) for z in range(1, outer)]
        plane = column + [across(0, y, count) ^ m for y in range(1, inner) for m in column]
    return plane + [m ^ 1 for m in plane]


def after_kernel(*refs):
    pass


def after(arrays, deps):
    arrays, deps = tuple(arrays), tuple(jax.tree.leaves(deps))
    return pl.pallas_call(
        after_kernel,
        out_shape=tuple(jax.ShapeDtypeStruct(x.shape, x.dtype) for x in arrays),
        in_specs=[ANY] * (len(arrays) + len(deps)),
        out_specs=(ANY,) * len(arrays),
        input_output_aliases={i: i for i in range(len(arrays))},
        compiler_params=pltpu.CompilerParams(vmem_limit_bytes=MIB),
        name="after",
    )(*arrays, *deps)


def gather(block, count, beside):
    outer, inner, _ = factors(count)
    to = lambda x, z, y: send(x, across(z, y, count), count)
    if (outer, inner) == (4, 2):
        far, near, side = to(block, 2, 0), to(block, 1, 0), to(block, 0, 1)
        side, both, far = after((side, jnp.concatenate([near, far], 0), far), beside)
        corner = to(side, 3, 0)
        pair = to(both, 0, 1)
        third = to(far, 1, 0)
        plane = [jnp.concatenate([block, both, side], 0), jnp.concatenate([third, corner], 0), pair]
    else:
        column = jnp.concatenate([block] + [to(block, z, 0) for z in range(1, outer)], 0)
        (column,) = after((column,), beside)
        plane = [column] + [to(column, 0, y) for y in range(1, inner)]
    return plane + [send(p, 1, count) for p in plane]


def owner_of(slot, me, masks):
    mask = jnp.zeros_like(slot)
    for i, m in enumerate(masks):
        mask = jnp.where(slot == i, m, mask)
    return me ^ mask


def lead_kernel(out_ref):
    out_ref[...] = jnp.zeros_like(out_ref)


def pack_kernel(lead_ref, parent_ref, token_ref, out_ref):
    width = token_ref.shape[1]
    half = width // 2
    out_ref[:, :width] = token_ref[...]
    row = parent_ref[...].astype(F32)
    out_ref[:, width:] = jnp.concatenate([row[:, :half], row[:, half:]], 0).astype(BF)


def pack(parent_rows, token_rows):
    width = token_rows.shape[1]
    lead = pl.pallas_call(
        lead_kernel,
        out_shape=jax.ShapeDtypeStruct((8, 128), F32),
        out_specs=VMEM,
        compiler_params=pltpu.CompilerParams(vmem_limit_bytes=4 * MIB),
        cost_estimate=LONG,
        name="lead",
    )()
    return pl.pallas_call(
        pack_kernel,
        out_shape=jax.ShapeDtypeStruct((2, width * 3 // 2), BF),
        in_specs=[VMEM] * 3,
        out_specs=VMEM,
        compiler_params=pltpu.CompilerParams(vmem_limit_bytes=4 * MIB),
        cost_estimate=LONG,
        name="pack",
    )(lead, parent_rows, token_rows)


def flip_kernel(w_ref, out_ref, flip_ref):
    out_ref[...] = w_ref[...]
    flip_ref[...] = w_ref[...].T


def flip(w):
    return pl.pallas_call(
        flip_kernel,
        out_shape=(jax.ShapeDtypeStruct(w.shape, BF), jax.ShapeDtypeStruct(w.shape[::-1], BF)),
        in_specs=[VMEM],
        out_specs=(VMEM,) * 2,
        compiler_params=pltpu.CompilerParams(vmem_limit_bytes=16 * MIB),
        cost_estimate=pl.CostEstimate(flops=0, bytes_accessed=4 * w.size, transcendentals=0),
        name="flip",
    )(w)


def select_kernel(count, me_ref, parent_ref, flow_ref, flow_out, pick_ref, sums_ref):
    hyp = parent_ref.shape[1]
    rows = 2 * count
    me = me_ref[0]
    line = lax.broadcasted_iota(jnp.int32, (hyp, hyp), 0)
    order = owner_of(line >> 1, me, gather_masks(count)) * 2 + (line & 1)
    perm = order == lax.broadcasted_iota(jnp.int32, (hyp, hyp), 1)
    flow_out[...] = jnp.dot(perm.astype(F32).astype(BF), flow_ref[...], preferred_element_type=F32)
    owner = jnp.sum(jnp.where(perm, parent_ref[...].astype(F32), 0.0), axis=1, keepdims=True)
    pair = lax.broadcasted_iota(jnp.int32, (hyp, rows), 1)

    def halves(masks):
        match = owner_of(pair >> 1, me, masks).astype(F32) == owner
        return [jnp.where(match & ((pair & 1) == side), 1.0, 0.0) for side in (0, 1)]

    pick_ref[...] = jnp.concatenate(halves(gather_masks(count)), 0).astype(BF)
    sums_ref[...] = jnp.concatenate([h.T for h in halves(scatter_masks(count))], 0).astype(BF)


def select(me, parent, d_hidden, count):
    hyp = parent.shape[0]
    return pl.pallas_call(
        functools.partial(select_kernel, count),
        out_shape=(
            jax.ShapeDtypeStruct(d_hidden.shape, F32),
            jax.ShapeDtypeStruct((2 * hyp, 2 * count), BF),
            jax.ShapeDtypeStruct((4 * count, hyp), BF),
        ),
        in_specs=[SMEM, VMEM, VMEM],
        out_specs=(VMEM,) * 3,
        compiler_params=pltpu.CompilerParams(vmem_limit_bytes=16 * MIB),
        name="select",
    )(me, parent.reshape(1, hyp), d_hidden)


def forward_kernel(columns, flow_ref, pick_ref, sums_ref, wg_ref, wu_ref, wgt_ref, wut_ref, *refs):
    cols, (x_ref, d_ref, own_ref, out_ref) = refs[:columns], refs[columns:]
    hyp = flow_ref.shape[0]
    width, hidden = wg_ref.shape
    half = width // 2
    rows = sums_ref.shape[0] // 2
    count = rows // 2

    step = half if count <= 16 else 1024
    for at in range(0, half, step):
        here, there, held = (pl.ds(at + base, step) for base in (0, half, width))
        pairs = jnp.concatenate([c[:, held].astype(F32) for c in cols], 0).astype(BF)
        picked = jnp.dot(pick_ref[...], pairs, preferred_element_type=F32)
        for top, sel in ((0, here), (hyp, there)):
            tokens = jnp.concatenate([c[:, sel].astype(F32) for c in cols], 0)
            x_ref[:, sel] = (picked[top:top + hyp] + tokens).astype(BF)

    gate = jnp.dot(x_ref[...], wg_ref[...], preferred_element_type=F32)
    up = jnp.dot(x_ref[...], wu_ref[...], preferred_element_type=F32)
    flow = flow_ref[...]
    sig = 1.0 / (1.0 + jnp.exp(-gate))
    d_gate = (flow * up * sig * (1.0 + gate * (1.0 - sig))).astype(BF)
    d_up = (flow * gate * sig).astype(BF)
    d = jnp.concatenate([d_gate, d_up], 1)
    d_ref[...] = d
    sums = jnp.dot(sums_ref[...], d, preferred_element_type=F32).astype(BF)
    even, odd = sums[:rows], sums[rows:]
    for at in range(0, half, step):
        here, there = pl.ds(at, step), pl.ds(at + half, step)
        term = jnp.dot(even[:, :hidden], wgt_ref[:, here], preferred_element_type=F32)
        term = term + jnp.dot(even[:, hidden:], wut_ref[:, here], preferred_element_type=F32)
        term = term + jnp.dot(odd[:, :hidden], wgt_ref[:, there], preferred_element_type=F32)
        term = term + jnp.dot(odd[:, hidden:], wut_ref[:, there], preferred_element_type=F32)
        own_ref[:, here] = term[:count]
        out_ref[:, here] = term[count:].astype(BF)


def forward(flow, pick, sums, w_gate, w_up, flip_gate, flip_up, columns):
    width, hidden = w_gate.shape
    hyp = flow.shape[0]
    count = sums.shape[0] // 4
    return pl.pallas_call(
        functools.partial(forward_kernel, len(columns)),
        out_shape=(
            jax.ShapeDtypeStruct((hyp, width), BF),
            jax.ShapeDtypeStruct((hyp, 2 * hidden), BF),
            jax.ShapeDtypeStruct((count, width // 2), F32),
            jax.ShapeDtypeStruct((count, width // 2), BF),
        ),
        in_specs=[VMEM] * (7 + len(columns)),
        out_specs=(VMEM,) * 4,
        compiler_params=pltpu.CompilerParams(vmem_limit_bytes=48 * MIB if count > 16 else 24 * MIB),
        cost_estimate=pl.CostEstimate(flops=8 * hyp * width * hidden, bytes_accessed=8 * width * hidden, transcendentals=hyp * hidden),
        name="forward",
    )(flow, pick, sums, w_gate, w_up, flip_gate, flip_up, *columns)


def weight_kernel(side, step, x_ref, d_ref, *refs):
    out_ref, done_ref, buf, sems = refs[-4:]
    over = (((0,), (0,)), ((), ()))
    hidden = out_ref.shape[1]
    copies = []
    for i in range(x_ref.shape[1] // step):
        rows = pl.ds(i * step, step)
        d = d_ref[:, side * hidden:(side + 1) * hidden]
        buf[rows, :] = lax.dot_general(x_ref[:, rows], d, over, preferred_element_type=F32).astype(BF)
        copies.append(pltpu.make_async_copy(buf.at[rows], out_ref.at[rows], sems.at[i]))
        copies[-1].start()
    done_ref[...] = jnp.zeros_like(done_ref)
    for copy in copies:
        copy.wait()


def weight_terms(x, d, side, *deps):
    hyp, width = x.shape
    hidden = d.shape[1] // 2
    step = 1024
    return pl.pallas_call(
        functools.partial(weight_kernel, side, step),
        out_shape=(jax.ShapeDtypeStruct((width, hidden), BF), jax.ShapeDtypeStruct((8, 128), F32)),
        in_specs=[VMEM] * 2 + [ANY] * len(deps),
        out_specs=(HBM, VMEM),
        scratch_shapes=[pltpu.VMEM((width, hidden), BF), pltpu.SemaphoreType.DMA((width // step,))],
        compiler_params=pltpu.CompilerParams(vmem_limit_bytes=24 * MIB),
        cost_estimate=pl.CostEstimate(flops=2 * hyp * width * hidden, bytes_accessed=2 * width * hidden, transcendentals=0),
        name="weight_terms",
    )(x, d, *deps)


def body(parent_rows, token_rows, parent, d_hidden, w_gate, w_up):
    count = lax.axis_size("blk")
    outer, inner, _ = factors(count)
    width = token_rows.shape[1]
    me = lax.axis_index("blk").reshape(1)

    block = pack(parent_rows, token_rows)
    beside = (select(me, parent, d_hidden, count), flip(w_gate), flip(w_up))
    columns = gather(block, count, beside)
    (flow, pick, sums), (w_gate, flip_gate), (w_up, flip_up) = beside
    x, d, own, other = forward(flow, pick, sums, w_gate, w_up, flip_gate, flip_up, columns)
    rows = own + send(other, 1, count).astype(F32)
    grad_gate, done = weight_terms(x, d, 0)
    stages = scatter_stages(count)[1:]
    for i, stage in enumerate(stages):
        size = rows.shape[0] // len(stage)
        parts = [rows[j * size:(j + 1) * size] for j in range(len(stage))]
        outgoing = [part.astype(BF) for part in parts[1:]]
        if i == len(stages) - 1:
            outgoing = after(outgoing, done)
            grad_up, done = weight_terms(x, d, 1, outgoing[0])
        arrived = [send(part, mask, count) for mask, part in zip(stage[1:], outgoing)]
        if i == len(stages) - 1:
            arrived = after(arrived, done)
        rows = parts[0]
        for part in arrived:
            rows = rows + part.astype(F32)
    return grad_gate, grad_up, rows.astype(BF).reshape(1, width)


def solution(mesh):
    in_specs = (
        P(("grp", "blk"), None),
        P(("grp", "blk"), None),
        P("grp"),
        P("grp", "blk"),
        P(None, "blk"),
        P(None, "blk"),
    )
    out_specs = (P(None, ("grp", "blk")), P(None, ("grp", "blk")), P(("grp", "blk"), None))
    return jax.shard_map(body, mesh=mesh, in_specs=in_specs, out_specs=out_specs, check_vma=False)
```
